32 devices in a mesh: groups: 2 (over x), seq: 16 (over z, y, core).
Axes of the slice: x: 2, y: 2, z: 4, core: 2. Of those that a mesh axis runs over, the one named last changes fastest.
Arguments:
- queries: bfloat16 [96, 8192], P(('groups', 'seq')), parts along dimension 0, may hold values from -48 to 48
- prompt_of: int32 [96, 1], P(('groups', 'seq')), parts along dimension 0, may hold values from 0 to 1; in each aligned block of 3 rows (0 to 2, 3 to 5, ...) at most 2 rows name the same one
- suffix_cache: bfloat16 [96, 512, 2048], P(('groups', 'seq')), parts along dimension 0, may hold values from -6 to 6
- suffix_blocks: int32 [96], P(('groups', 'seq')), parts along dimension 0, may hold values from 1 to 4
- prompt_cache: bfloat16 [4, 2048, 2048], P('groups', 'seq'), parts along dimension 0, may hold values from -16 to 16
- reward_weight: float32 [8192], replicated, may hold values from -0.4375 to 0.4375
Outputs:
- attended: bfloat16 [96, 8192], P(('groups', 'seq')), parts along dimension 0
- scores: float32 [96], P(('groups', 'seq')), parts along dimension 0
The draws below stay inside these ranges and needn't reach their ends.
There are 2 independent parts, one for each index of `groups`. The reference program is written for one: setup_inputs(seed, part) draws one part's arguments, and reference() takes and returns one part's arrays. A program takes and returns all parts, laid end to end along the dimension named above; an argument that names none is the same for every part. Nothing has to cross between parts.
Inputs may be any that keep to these rules, and one draw needn't show every extreme that they name: `prompt_of`: in each device's aligned block of 3 rows at most 2 candidates name the same prompt.
All inputs are finite; a program needn't handle non-finite values.
Results may differ from the reference program's by a relative error of at most 0.015.
Values may be sent and summed in bfloat16 or wider, within the bound.
A program may use at most 192 MiB of HBM per device.

```python
import math
import jax
import jax.numpy as jnp
import numpy as np
from jax import lax

HQ = 64
KVH = 8
HD = 128
PROMPT_DEV = 128
PROMPTS = 2
CAND_DEV = 3
CAP = 2
BLOCK = 128
SUF_BLOCKS = 4
CANDS = 48
PROMPT_LEN = 2048
SUF_MAX = 512
N_SEQ = 16


def draw_queries(key, part):
    drawn = jax.random.normal(jax.random.fold_in(key, 101), (CANDS, HQ * HD), jnp.float32)
    return jnp.clip(3.0 * drawn, -15.0, 15.0).astype(jnp.bfloat16)


def draw_prompt_cache(key, part):
    drawn = jnp.clip(jax.random.normal(jax.random.fold_in(key, 202), (PROMPTS, PROMPT_LEN, 2 * KVH * HD), jnp.float32), -6.0, 6.0)
    return drawn.astype(jnp.bfloat16)


def draw_suffix_blocks(key, part):
    counts = jax.random.randint(jax.random.fold_in(key, 303), (CANDS,), 1, SUF_BLOCKS + 1, dtype=jnp.int32)
    return counts.at[0].set(SUF_BLOCKS)


def block_levels(own_key, shape, pieces, low, top_value):
    def one(position, parts):
        draws = jax.random.uniform(jax.random.fold_in(jax.random.fold_in(own_key, 6), position), (parts,), jnp.float32, low / len(pieces), top_value / len(pieces))
        return jnp.repeat(jnp.exp(draws), shape[position] // parts).reshape((-1,) + (1,) * (len(shape) - position - 1))

    loudness = one(*pieces[0])
    for cut in pieces[1:]:
        loudness = loudness * one(*cut)
    return loudness


def routed_block(key, own, number, rows, count, top, reach, skew):
    sequence = jax.random.permutation(key, count)
    packed, usual = load_shares(count, rows * top, reach, skew, True), load_shares(count, rows * top, reach, skew, False)
    places = jnp.arange(count)

    def named(sizes, offset_by):
        used = int((sizes > 0).sum())
        fixed = max(1, used // 4)
        shifted = fixed + (places - fixed + offset_by * (used - fixed)) % max(1, count - fixed)
        return jnp.zeros((count,), jnp.int32).at[sequence[jnp.where(places < fixed, places, shifted)]].set(jnp.asarray(sizes, jnp.int32))

    sizes = jnp.where(number % 4 == 0, named(packed, number // 4), named(usual, number - number // 4 - 1))
    mixed = jax.random.permutation(jax.random.fold_in(own, 3), count)
    source_of, taker = mixed[0:count // 2 * 2:2], mixed[1:count // 2 * 2:2]
    room = jnp.minimum(sizes[source_of] - 1, reach - sizes[taker]) // 2
    room = jnp.where((source_of == sequence[0]) | (taker == sequence[0]) | (sizes[taker] == 0), 0, jnp.maximum(room, 0))
    shifted = jax.random.randint(jax.random.fold_in(own, 4), (count // 2,), 0, 1 << 20) % (room + 1)
    sizes = sizes.at[source_of].add(-shifted).at[taker].add(shifted)
    items = jnp.searchsorted(jnp.cumsum(sizes), jnp.arange(rows * top), side="right").astype(jnp.int32)
    grid = items.reshape(top, rows).T
    grid = grid[jax.random.permutation(jax.random.fold_in(own, 1), rows)]
    offset_by = jax.random.randint(jax.random.fold_in(own, 2), (rows, 1), 0, top)
    return jnp.take_along_axis(grid, (jnp.arange(top)[None, :] + offset_by) % top, axis=1)


def load_shares(amount, total, limit, lean, full):
    weights = [(1 << 20) // math.isqrt(standing ** lean) + 1 for standing in range(1, amount + 1)]
    largest = limit if full else min(limit, max(-(-total // amount), total * weights[0] // sum(weights)))
    least = 1 if total - largest >= amount - 1 else 0
    given, rest = [largest] + [least] * (amount - 1), total - largest - least * (amount - 1)
    while rest > 0:
        free = [i for i in range(1, amount) if given[i] < largest] or [i for i in range(1, amount) if given[i] < limit]
        pool, budget = sum([weights[i] for i in free]), rest
        for i in free:
            extra = min(limit - given[i], max(1, budget * weights[i] // pool), rest)
            given[i] = given[i] + extra
            rest = rest - extra
    return np.array(given)


def noise(rng, dims, spread, limit, cuts=(), kind=jnp.bfloat16):
    entries = spread * jax.random.normal(rng, dims, jnp.float32)
    if cuts:
        entries = entries * block_levels(rng, dims, cuts, -0.22, 0.18)
    return jnp.clip(entries, -limit, limit).astype(kind)


def setup_inputs(seed: int = 0, part: int = 0) -> dict:
    streams_of = jax.random.split(jax.random.key(seed), 7)
    part_splits = jax.random.split(jax.random.fold_in(streams_of[6], part), 7)
    queries = draw_queries(jax.random.fold_in(jax.random.fold_in(streams_of[6], part), 71), part)
    prompt_of_keys = jax.random.split(jax.random.fold_in(part_splits[1], 1), CANDS // CAND_DEV)
    prompt_of_turns = jax.random.permutation(jax.random.fold_in(part_splits[1], 3), CANDS // CAND_DEV)
    prompt_of = jax.vmap(lambda own, number: routed_block(jax.random.fold_in(part_splits[1], 2), own, number, CAND_DEV, PROMPTS, 1, CAP, 1))(prompt_of_keys, prompt_of_turns).reshape((CANDS, 1))
    suffix_cache = noise(part_splits[2], (CANDS, SUF_MAX, 2 * KVH * HD), 1.3, 6.0, ((0, 16),))
    suffix_blocks = draw_suffix_blocks(jax.random.fold_in(jax.random.fold_in(streams_of[6], part), 71), part)
    prompt_cache = draw_prompt_cache(jax.random.fold_in(jax.random.fold_in(streams_of[6], part), 71), part)
    reward_weight = noise(streams_of[5], (HQ * HD,), 0.03, 0.4375, (), jnp.float32)
    return {"queries": queries, "prompt_of": prompt_of, "suffix_cache": suffix_cache, "suffix_blocks": suffix_blocks, "prompt_cache": prompt_cache, "reward_weight": reward_weight}


floor_logit = -1.0e30


def merge_parts(first, second):
    joined = jnp.maximum(first[0], second[0])
    keep = jnp.exp(first[0] - joined)
    take = jnp.exp(second[0] - joined)
    sums = first[1] * keep + second[1] * take
    row_count, heads = joined.shape
    mixes = first[2].reshape(row_count, heads, -1) * keep[:, :, None] + second[2].reshape(row_count, heads, -1) * take[:, :, None]
    return (joined, sums, mixes.reshape(row_count, -1))


def prompt_part(grouped, block_cache):
    kv_width = KVH * HD
    keys = block_cache[:, :kv_width].astype(jnp.float32).reshape(-1, KVH, HD)
    values = block_cache[:, kv_width:].astype(jnp.float32).reshape(-1, KVH, HD)
    logits = jnp.einsum("ckgd,tkd->ckgt", grouped, keys) * (HD ** -0.5)
    maxima = jnp.max(logits, axis=-1)
    exponent = jnp.exp(logits - maxima[..., None])
    totals = jnp.sum(exponent, axis=-1)
    rounded = lax.optimization_barrier(exponent.astype(jnp.bfloat16))
    weights = rounded.astype(jnp.float32)
    weighted = jnp.einsum("ckgt,tkd->ckgd", weights, values)
    row_count = grouped.shape[0]
    return (maxima.reshape(row_count, -1), totals.reshape(row_count, -1), weighted.reshape(row_count, -1))


def suffix_part(item_triple):
    query_row, cache_rows, block_count = item_triple
    kv_width = KVH * HD
    grouped = query_row.astype(jnp.float32).reshape(KVH, HQ // KVH, HD)
    keys = cache_rows[:, :kv_width].astype(jnp.float32).reshape(SUF_MAX, KVH, HD)
    values = cache_rows[:, kv_width:].astype(jnp.float32).reshape(SUF_MAX, KVH, HD)
    logits = jnp.einsum("kgd,tkd->kgt", grouped, keys) * (HD ** -0.5)
    live_mask = (jnp.arange(SUF_MAX, dtype=jnp.int32) < BLOCK * block_count)[None, None, :]
    logits = jnp.where(live_mask, logits, floor_logit)
    maxima = jnp.max(logits, axis=-1)
    exponent = jnp.where(live_mask, jnp.exp(logits - maxima[..., None]), 0.0)
    totals = jnp.sum(exponent, axis=-1)
    rounded = lax.optimization_barrier(exponent.astype(jnp.bfloat16))
    weights = rounded.astype(jnp.float32)
    weighted = jnp.einsum("kgt,tkd->kgd", weights, values)
    return (maxima.reshape(-1), totals.reshape(-1), weighted.reshape(-1))


def reference(queries, prompt_of, suffix_cache, suffix_blocks, prompt_cache, reward_weight):
    cand_rows = queries.shape[0]
    start_state = lax.map(suffix_part, (queries, suffix_cache, suffix_blocks))
    grouped = queries.astype(jnp.float32).reshape(cand_rows, KVH, HQ // KVH, HD)
    prompt_ids = prompt_of[:, 0]

    def visit_block(carried, block_index):
        start_row = (block_index * PROMPT_DEV).astype(jnp.int32)
        block_cache = lax.dynamic_slice_in_dim(prompt_cache, start_row, PROMPT_DEV, axis=1)
        chosen = prompt_part(grouped, block_cache[0])
        for prompt in range(1, PROMPTS):
            partial_value = prompt_part(grouped, block_cache[prompt])
            picked = (prompt_ids == prompt)[:, None]
            chosen = tuple(jnp.where(picked, fresh_part, older_part) for fresh_part, older_part in zip(partial_value, chosen))
        return merge_parts(carried, chosen), None

    final_state, unused = lax.scan(visit_block, start_state, jnp.arange(N_SEQ, dtype=jnp.int32))
    attended_full = final_state[2].reshape(cand_rows, HQ, HD) / final_state[1][:, :, None]
    attended = attended_full.reshape(cand_rows, -1).astype(jnp.bfloat16)
    scores = jnp.sum(attended.astype(jnp.float32) * reward_weight, axis=-1)
    return (attended, scores)
```

```python
import functools
import math

import jax
import jax.numpy as jnp
from jax import lax
from jax.experimental import pallas as pl
from jax.experimental.pallas import tpu as pltpu
from jax.sharding import PartitionSpec as P

HD = 128
BLOCK = 128
CORES = 2
FLOOR = -1e30
MESH = pl.DeviceIdType.MESH
F32 = jnp.float32
BF16 = jnp.bfloat16


def to_lanes(columns):
    rows = columns[0].shape[0]
    lane = lax.broadcasted_iota(jnp.int32, (rows, 128), 1)
    tile = jnp.zeros((rows, 128), F32)
    for index, column in enumerate(columns):
        tile = jnp.where(lane == index, column, tile)
    if rows < 128:
        tile = jnp.concatenate([tile, jnp.zeros((128 - rows, 128), F32)], axis=0)
    return jnp.transpose(tile)[:8]


def to_columns(lanes, rows):
    count = lanes.shape[0]
    tile = jnp.concatenate([lanes, jnp.zeros((128 - count, 128), F32)], axis=0)
    return jnp.transpose(tile)[:rows]


def kernel(
    sizes,
    q_ref,
    blocks_ref,
    weight_ref,
    prompt_hbm,
    suffix_hbm,
    out_ref,
    score_ref,
    kbuf,
    vbuf,
    sbuf,
    qbuf,
    own_mix,
    own_stat,
    y_mix,
    y_stat,
    y_mix_in,
    y_stat_in,
    z_mix,
    z_stat,
    z_mix_in,
    z_stat_in,
    suf_mix,
    suf_stat,
    kv_local,
    kv_send,
    kv_recv,
    suf_sem,
    qz_send,
    qz_recv,
    qy_send,
    qy_recv,
    ym_send,
    ym_recv,
    ys_send,
    ys_recv,
    zm_send,
    zm_recv,
    zs_send,
    zs_recv,
):
    A, B, cands, kv_heads, group = sizes
    half_heads = kv_heads // CORES
    piece = cands * group
    rows = half_heads * piece
    half_width = half_heads * HD
    kv_width = kv_heads * HD
    span = prompt_hbm.shape[1]
    prompts = prompt_hbm.shape[0]
    scale = HD**-0.5

    me = lax.axis_index("seq")
    c = lax.rem(me, CORES)
    y = lax.rem(me // CORES, B)
    z = me // (CORES * B)
    other = 1 - c

    def device(zz, yy, cc):
        return {"seq": (zz * B + yy) * CORES + cc}

    local = []
    for index, (buf, base) in enumerate(((kbuf, 0), (vbuf, kv_width))):
        copy = pltpu.make_async_copy(
            prompt_hbm.at[:, :, pl.ds(pl.multiple_of(base + c * half_width, 128), half_width)],
            buf.at[:, pl.ds(0, span), :],
            kv_local.at[index],
        )
        copy.start()
        local.append(copy)
    suffix_copies = []
    for cand in range(cands):
        copy = pltpu.make_async_copy(suffix_hbm.at[cand], sbuf.at[cand], suf_sem.at[cand])
        copy.start()
        suffix_copies.append(copy)

    barrier = pltpu.get_barrier_semaphore()
    pl.semaphore_signal(barrier, inc=1, device_id=device(z, y, other), device_id_type=MESH)
    for off in range(1, A):
        zz = lax.rem(z + off, A)
        for cc in range(CORES):
            pl.semaphore_signal(barrier, inc=1, device_id=device(zz, y, cc), device_id_type=MESH)
    for off in range(1, B):
        yy = lax.rem(y + off, B)
        pl.semaphore_signal(barrier, inc=1, device_id=device(z, yy, c), device_id_type=MESH)
    pl.semaphore_wait(barrier, 1 + CORES * (A - 1) + (B - 1))

    def q_copy(zz, cc, from_z, from_c):
        return pltpu.make_async_remote_copy(
            src_ref=q_ref.at[cc],
            dst_ref=qbuf.at[y, from_z, from_c],
            send_sem=qz_send.at[zz, cc],
            recv_sem=qz_recv.at[from_z, from_c],
            device_id=device(zz, y, cc),
            device_id_type=MESH,
        )

    q_copy(z, other, z, c).start()
    for off in range(1, A):
        zz = lax.rem(z + off, A)
        for cc in range(CORES):
            q_copy(zz, cc, z, c).start()
    qbuf[y, z, c] = q_ref[c]

    def kv_copy(index, buf, base):
        return pltpu.make_async_remote_copy(
            src_ref=prompt_hbm.at[
                :, :, pl.ds(pl.multiple_of(base + other * half_width, 128), half_width)
            ],
            dst_ref=buf.at[:, pl.ds(span, span), :],
            send_sem=kv_send.at[index],
            recv_sem=kv_recv.at[index],
            device_id=device(z, y, other),
            device_id_type=MESH,
        )

    kv_copies = [kv_copy(0, kbuf, 0), kv_copy(1, vbuf, kv_width)]
    for copy in kv_copies:
        copy.start()

    def y_copy(zz, yy, from_y):
        return pltpu.make_async_remote_copy(
            src_ref=qbuf.at[y, zz],
            dst_ref=qbuf.at[from_y, zz],
            send_sem=qy_send.at[yy, zz],
            recv_sem=qy_recv.at[from_y, zz],
            device_id=device(z, yy, c),
            device_id_type=MESH,
        )

    def forward(off):
        zz = lax.rem(z + off, A)
        if off == 0:
            q_copy(z, other, z, other).wait_recv()
        else:
            for cc in range(CORES):
                q_copy(zz, cc, zz, cc).wait_recv()
        for step in range(1, B):
            yy = lax.rem(y + step, B)
            y_copy(zz, yy, y).start()

    length = sbuf.shape[1]
    position = lax.broadcasted_iota(jnp.int32, (group, length), 1)

    def suffix(cand):
        suffix_copies[cand].wait()
        live = position < BLOCK * blocks_ref[cand]
        for head in range(kv_heads):
            side, inner = head // half_heads, head % half_heads
            start = inner * piece + cand * group
            query = q_ref[side].astype(F32)[start : start + group].astype(BF16)
            keys = sbuf[cand, :, head * HD : (head + 1) * HD]
            values = sbuf[cand, :, kv_width + head * HD : kv_width + (head + 1) * HD]
            logits = (
                lax.dot_general(query, keys, (((1,), (1,)), ((), ())), preferred_element_type=F32)
                * scale
            )
            logits = jnp.where(live, logits, FLOOR)
            top = jnp.max(logits, axis=1, keepdims=True)
            weights = jnp.where(live, jnp.exp(logits - top), 0.0)
            total = jnp.sum(weights, axis=1, keepdims=True)
            suf_mix[side, start : start + group, :] = jnp.dot(
                weights.astype(BF16), values, preferred_element_type=F32
            )
            suf_stat[side, 0, start : start + group, :] = jnp.broadcast_to(top, (group, 128))
            suf_stat[side, 1, start : start + group, :] = jnp.broadcast_to(total, (group, 128))

    forward(0)
    order = list(range(1, A))
    for cand in range(cands):
        suffix(cand)
        if cand < len(order):
            forward(order[cand])
    for off in order[cands:]:
        forward(off)

    for copy in local:
        copy.wait()
    for copy in kv_copies:
        copy.wait()

    def attend(yy, zz):
        packets = [qbuf[yy, zz, cc].astype(F32) for cc in range(CORES)]
        marks = jnp.concatenate(
            [
                jnp.broadcast_to(packets[cc][rows + cand : rows + cand + 1], (group, 128))
                for cc in range(CORES)
                for cand in range(cands)
            ],
            axis=0,
        )
        marks = jnp.concatenate([marks] * (CORES * span // 128), axis=1)
        tops, totals, mixes = [], [], []
        for head in range(half_heads):
            query = jnp.concatenate(
                [packets[cc][head * piece : (head + 1) * piece] for cc in range(CORES)], axis=0
            ).astype(BF16)
            lanes = slice(head * HD, (head + 1) * HD)
            logits = None
            for prompt in range(prompts):
                part = lax.dot_general(
                    query,
                    kbuf[prompt, :, lanes],
                    (((1,), (1,)), ((), ())),
                    preferred_element_type=F32,
                )
                logits = part if prompt == 0 else jnp.where(marks == prompt, part, logits)
            logits = logits * scale
            top = jnp.max(logits, axis=1, keepdims=True)
            weights = jnp.exp(logits - top)
            totals.append(jnp.sum(weights, axis=1, keepdims=True))
            tops.append(top)
            mix = None
            for prompt in range(prompts):
                part = jnp.dot(
                    jnp.where(marks == prompt, weights, 0.0).astype(BF16),
                    vbuf[prompt, :, lanes],
                    preferred_element_type=F32,
                )
                mix = part if mix is None else mix + part
            mixes.append(mix)

        def side(parts, cc):
            return jnp.concatenate([p[cc * piece : (cc + 1) * piece] for p in parts], axis=0)

        stat = to_lanes([side(tops, 0), side(tops, 1), side(totals, 0), side(totals, 1)])
        return stat, [side(mixes, cc) for cc in range(CORES)]

    def own(off, carry):
        zz = lax.rem(z + off, A)
        stat, mixes = attend(y, zz)
        own_stat[zz] = stat
        for cc in range(CORES):
            own_mix[zz, cc] = mixes[cc]
        return carry

    lax.fori_loop(0, A, own, 0)

    def ym_copy(zz, yy, from_y):
        return pltpu.make_async_remote_copy(
            src_ref=y_mix.at[yy, zz],
            dst_ref=y_mix_in.at[from_y, zz],
            send_sem=ym_send.at[yy, zz],
            recv_sem=ym_recv.at[from_y, zz],
            device_id=device(z, yy, c),
            device_id_type=MESH,
        )

    def ys_copy(zz, yy, from_y):
        return pltpu.make_async_remote_copy(
            src_ref=y_stat.at[yy, zz],
            dst_ref=y_stat_in.at[from_y, zz],
            send_sem=ys_send.at[yy, zz],
            recv_sem=ys_recv.at[from_y, zz],
            device_id=device(z, yy, c),
            device_id_type=MESH,
        )

    def helped(off, carry):
        zz = lax.rem(z + off, A)
        for step in range(1, B):
            yy = lax.rem(y + step, B)
            y_copy(zz, yy, yy).wait_recv()
            stat, mixes = attend(yy, zz)
            y_stat[yy, zz] = stat
            for cc in range(CORES):
                y_mix[yy, zz, cc] = mixes[cc].astype(BF16)
            ym_copy(zz, yy, y).start()
            ys_copy(zz, yy, y).start()
        return carry

    lax.fori_loop(0, A, helped, 0)

    def zm_copy(zz, cc, from_z, from_c):
        return pltpu.make_async_remote_copy(
            src_ref=z_mix.at[zz, cc],
            dst_ref=z_mix_in.at[from_z, from_c],
            send_sem=zm_send.at[zz, cc],
            recv_sem=zm_recv.at[from_z, from_c],
            device_id=device(zz, y, cc),
            device_id_type=MESH,
        )

    def zs_copy(zz, cc, from_z, from_c):
        return pltpu.make_async_remote_copy(
            src_ref=z_stat.at[zz, cc],
            dst_ref=z_stat_in.at[from_z, from_c],
            send_sem=zs_send.at[zz, cc],
            recv_sem=zs_recv.at[from_z, from_c],
            device_id=device(zz, y, cc),
            device_id_type=MESH,
        )

    def merged(zz):
        for step in range(1, B):
            yy = lax.rem(y + step, B)
            ym_copy(zz, yy, yy).wait_recv()
            ys_copy(zz, yy, yy).wait_recv()
        stats = [own_stat[zz]]
        for step in range(1, B):
            stats.append(y_stat_in[lax.rem(y + step, B), zz])
        top = functools.reduce(jnp.maximum, [s[0:2] for s in stats])
        factors = [jnp.exp(s[0:2] - top) for s in stats]
        total = sum(f * s[2:4] for f, s in zip(factors, stats))
        columns = to_columns(jnp.concatenate(factors, axis=0), rows)
        results = []
        for cc in range(CORES):
            mix = own_mix[zz, cc] * columns[:, cc : cc + 1]
            for step in range(1, B):
                arrived = y_mix_in[lax.rem(y + step, B), zz, cc].astype(F32)
                index = step * CORES + cc
                mix = mix + arrived * columns[:, index : index + 1]
            stat = jnp.concatenate(
                [top[cc : cc + 1], total[cc : cc + 1], jnp.zeros((6, 128), F32)], axis=0
            )
            results.append((mix.astype(BF16), stat))
        return results

    def returned(off, carry):
        zz = lax.rem(z + off, A)
        for cc, (mix, stat) in enumerate(merged(zz)):
            z_mix[zz, cc] = mix
            z_stat[zz, cc] = stat
            zm_copy(zz, cc, z, c).start()
            zs_copy(zz, cc, z, c).start()
        return carry

    lax.fori_loop(1, A, returned, 0)
    for cc, (mix, stat) in enumerate(merged(z)):
        z_mix[z, cc] = mix
        z_stat[z, cc] = stat
    zm_copy(z, other, z, c).start()
    zs_copy(z, other, z, c).start()
    z_mix_in[z, c] = z_mix[z, c]
    z_stat_in[z, c] = z_stat[z, c]

    zm_copy(z, other, z, other).wait_recv()
    zs_copy(z, other, z, other).wait_recv()
    for off in range(1, A):
        zz = lax.rem(z + off, A)
        for cc in range(CORES):
            zm_copy(zz, cc, zz, cc).wait_recv()
            zs_copy(zz, cc, zz, cc).wait_recv()

    scores = [0.0] * cands
    for side in range(CORES):
        suf = to_lanes([suf_stat[side, 0][:, 0:1], suf_stat[side, 1][:, 0:1]])
        stats = [z_stat_in[zz, side] for zz in range(A)] + [suf]
        top = functools.reduce(jnp.maximum, [s[0:1] for s in stats])
        factors = [jnp.exp(s[0:1] - top) for s in stats]
        total = sum(f * s[1:2] for f, s in zip(factors, stats))
        total = jnp.where(total > 0.0, total, 1.0)
        columns = to_columns(jnp.concatenate([f / total for f in factors], axis=0), rows)
        mix = suf_mix[side] * columns[:, A : A + 1]
        for zz in range(A):
            mix = mix + z_mix_in[zz, side].astype(F32) * columns[:, zz : zz + 1]
        half_rows = half_heads * group
        for cand in range(cands):
            picked = jnp.concatenate(
                [
                    mix[head * piece + cand * group : head * piece + (cand + 1) * group]
                    for head in range(half_heads)
                ],
                axis=0,
            ).astype(BF16)
            out_ref[cand, side * half_rows : (side + 1) * half_rows, :] = picked
            term = picked.astype(F32) * weight_ref[side * half_rows : (side + 1) * half_rows]
            scores[cand] = scores[cand] + jnp.sum(term)
    row = lax.broadcasted_iota(jnp.int32, (8, 128), 0)
    tile = jnp.zeros((8, 128), F32)
    for cand in range(cands):
        tile = jnp.where(row == cand, scores[cand], tile)
    score_ref[...] = tile

    q_copy(z, other, z, c).wait_send()
    zm_copy(z, other, z, c).wait_send()
    zs_copy(z, other, z, c).wait_send()

    def drain_z(off, carry):
        zz = lax.rem(z + off, A)
        for cc in range(CORES):
            q_copy(zz, cc, z, c).wait_send()
            zm_copy(zz, cc, z, c).wait_send()
            zs_copy(zz, cc, z, c).wait_send()
        return carry

    lax.fori_loop(1, A, drain_z, 0)

    def drain_y(zz, carry):
        for step in range(1, B):
            yy = lax.rem(y + step, B)
            y_copy(zz, yy, y).wait_send()
            ym_copy(zz, yy, y).wait_send()
            ys_copy(zz, yy, y).wait_send()
        return carry

    lax.fori_loop(0, A, drain_y, 0)


def body(A, B, queries, prompt_of, suffix_cache, suffix_blocks, prompt_cache, reward_weight):
    cands = queries.shape[0]
    heads = queries.shape[1] // HD
    prompts, span, width = prompt_cache.shape
    kv_heads = width // 2 // HD
    group = heads // kv_heads
    half_heads = kv_heads // CORES
    rows = half_heads * cands * group
    packet = rows + 16
    half_width = half_heads * HD

    ordered = queries.reshape(cands, CORES, half_heads, group, HD).transpose(1, 2, 0, 3, 4)
    ordered = ordered.reshape(CORES, rows, HD)
    marks = jnp.pad(prompt_of.astype(BF16), ((0, 16 - cands), (0, 0)))
    marks = jnp.broadcast_to(marks[None], (CORES, 16, HD))
    packed = jnp.concatenate([ordered, marks], axis=1)
    dma = pltpu.SemaphoreType.DMA

    attended, scores = pl.pallas_call(
        functools.partial(kernel, (A, B, cands, kv_heads, group)),
        out_shape=(
            jax.ShapeDtypeStruct((cands, heads, HD), BF16),
            jax.ShapeDtypeStruct((8, 128), F32),
        ),
        in_specs=[
            pl.BlockSpec(memory_space=pltpu.VMEM),
            pl.BlockSpec(memory_space=pltpu.SMEM),
            pl.BlockSpec(memory_space=pltpu.VMEM),
            pl.BlockSpec(memory_space=pl.ANY),
            pl.BlockSpec(memory_space=pl.ANY),
        ],
        out_specs=(
            pl.BlockSpec(memory_space=pltpu.VMEM),
            pl.BlockSpec(memory_space=pltpu.VMEM),
        ),
        scratch_shapes=[
            pltpu.VMEM((prompts, CORES * span, half_width), BF16),
            pltpu.VMEM((prompts, CORES * span, half_width), BF16),
            pltpu.VMEM(suffix_cache.shape, BF16),
            pltpu.VMEM((B, A, CORES, packet, HD), BF16),
            pltpu.VMEM((A, CORES, rows, HD), F32),
            pltpu.VMEM((A, 8, 128), F32),
            pltpu.VMEM((B, A, CORES, rows, HD), BF16),
            pltpu.VMEM((B, A, 8, 128), F32),
            pltpu.VMEM((B, A, CORES, rows, HD), BF16),
            pltpu.VMEM((B, A, 8, 128), F32),
            pltpu.VMEM((A, CORES, rows, HD), BF16),
            pltpu.VMEM((A, CORES, 8, 128), F32),
            pltpu.VMEM((A, CORES, rows, HD), BF16),
            pltpu.VMEM((A, CORES, 8, 128), F32),
            pltpu.VMEM((CORES, rows, HD), F32),
            pltpu.VMEM((CORES, 2, rows, 128), F32),
            dma((2,)),
            dma((2,)),
            dma((2,)),
            dma((cands,)),
            dma((A, CORES)),
            dma((A, CORES)),
            dma((B, A)),
            dma((B, A)),
            dma((B, A)),
            dma((B, A)),
            dma((B, A)),
            dma((B, A)),
            dma((A, CORES)),
            dma((A, CORES)),
            dma((A, CORES)),
            dma((A, CORES)),
        ],
        compiler_params=pltpu.CompilerParams(
            collective_id=0, has_side_effects=True, vmem_limit_bytes=48 * 1024 * 1024
        ),
    )(packed, suffix_blocks, reward_weight.reshape(heads, HD), prompt_cache, suffix_cache)
    return attended.reshape(cands, heads * HD), scores[:cands, 0]


def solution(mesh):
    chips = mesh.shape["seq"] // CORES
    B = 1
    while B * B * 4 <= chips and chips % (B * 2) == 0:
        B *= 2
    A = chips // B
    placed = (
        P(("groups", "seq"), None),
        P(("groups", "seq"), None),
        P(("groups", "seq"), None, None),
        P(("groups", "seq")),
        P("groups", "seq", None),
        P(),
    )
    return jax.shard_map(
        functools.partial(body, A, B),
        mesh=mesh,
        in_specs=placed,
        out_specs=(P(("groups", "seq"), None), P(("groups", "seq"))),
        check_vma=False,
    )
```

```python
import functools
import math

import jax
import jax.numpy as jnp
from jax import lax
from jax.experimental import pallas as pl
from jax.experimental.pallas import tpu as pltpu
from jax.sharding import PartitionSpec as P

HD = 128
BLOCK = 128
CORES = 2
FLOOR = -1e30
MESH = pl.DeviceIdType.MESH
F32 = jnp.float32
BF16 = jnp.bfloat16


def to_lanes(columns):
    rows = columns[0].shape[0]
    lane = lax.broadcasted_iota(jnp.int32, (rows, 128), 1)
    tile = jnp.zeros((rows, 128), F32)
    for index, column in enumerate(columns):
        tile = jnp.where(lane == index, column, tile)
    if rows < 128:
        tile = jnp.concatenate([tile, jnp.zeros((128 - rows, 128), F32)], axis=0)
    return jnp.transpose(tile)[:8]


def to_columns(lanes, rows):
    count = lanes.shape[0]
    tile = jnp.concatenate([lanes, jnp.zeros((128 - count, 128), F32)], axis=0)
    return jnp.transpose(tile)[:rows]


def kernel(
    sizes,
    q_hbm,
    ids_hbm,
    blocks_hbm,
    weight_hbm,
    prompt_hbm,
    suffix_hbm,
    out_ref,
    score_ref,
    q_raw,
    q_ref,
    ids_ref,
    blocks_ref,
    weight_ref,
    small_sem,
    kbuf,
    vbuf,
    sbuf,
    qbuf,
    own_mix,
    own_stat,
    y_mix,
    y_stat,
    y_mix_in,
    y_stat_in,
    z_mix,
    z_stat,
    z_mix_in,
    z_stat_in,
    suf_mix,
    suf_stat,
    kv_local,
    kv_send,
    kv_recv,
    suf_sem,
    qz_send,
    qz_recv,
    qy_send,
    qy_recv,
    ym_send,
    ym_recv,
    ys_send,
    ys_recv,
    zm_send,
    zm_recv,
    zs_send,
    zs_recv,
):
    A, B, cands, kv_heads, group = sizes
    half_heads = kv_heads // CORES
    piece = cands * group
    rows = half_heads * piece
    half_width = half_heads * HD
    kv_width = kv_heads * HD
    span = prompt_hbm.shape[1]
    prompts = prompt_hbm.shape[0]
    scale = HD**-0.5

    me = lax.axis_index("seq")
    c = lax.rem(me, CORES)
    y = lax.rem(me // CORES, B)
    z = me // (CORES * B)
    other = 1 - c

    def device(zz, yy, cc):
        return {"seq": (zz * B + yy) * CORES + cc}

    small = []
    for index, (src, dst) in enumerate(
        (
            (q_hbm, q_raw),
            (ids_hbm, ids_ref),
            (blocks_hbm, blocks_ref),
            (weight_hbm, weight_ref),
        )
    ):
        copy = pltpu.make_async_copy(src, dst, small_sem.at[index])
        copy.start()
        small.append(copy)
    local = []
    for index, (buf, base) in enumerate(((kbuf, 0), (vbuf, kv_width))):
        copy = pltpu.make_async_copy(
            prompt_hbm.at[:, :, pl.ds(pl.multiple_of(base + c * half_width, 128), half_width)],
            buf.at[:, pl.ds(0, span), :],
            kv_local.at[index],
        )
        copy.start()
        local.append(copy)
    suffix_copies = []
    for cand in range(cands):
        copy = pltpu.make_async_copy(suffix_hbm.at[cand], sbuf.at[cand], suf_sem.at[cand])
        copy.start()
        suffix_copies.append(copy)

    barrier = pltpu.get_barrier_semaphore()
    pl.semaphore_signal(barrier, inc=1, device_id=device(z, y, other), device_id_type=MESH)
    for off in range(1, A):
        zz = lax.rem(z + off, A)
        for cc in range(CORES):
            pl.semaphore_signal(barrier, inc=1, device_id=device(zz, y, cc), device_id_type=MESH)
    for off in range(1, B):
        yy = lax.rem(y + off, B)
        pl.semaphore_signal(barrier, inc=1, device_id=device(z, yy, c), device_id_type=MESH)

    small[0].wait()
    small[1].wait()
    raw = q_raw[...].astype(F32)
    by_head = [raw[cand : cand + 1].reshape(kv_heads * group, HD) for cand in range(cands)]
    row = lax.broadcasted_iota(jnp.int32, (16, HD), 0)
    marked = jnp.zeros((16, HD), F32)
    for cand in range(cands):
        marked = jnp.where(row == cand, ids_ref[0, cand].astype(F32), marked)
    for side in range(CORES):
        pieces = [
            by_head[cand][(side * half_heads + head) * group :][:group]
            for head in range(half_heads)
            for cand in range(cands)
        ]
        q_ref[side] = jnp.concatenate(pieces + [marked], axis=0).astype(BF16)
    small[2].wait()
    small[3].wait()
    pl.semaphore_wait(barrier, 1 + CORES * (A - 1) + (B - 1))

    def q_copy(zz, cc, from_z, from_c):
        return pltpu.make_async_remote_copy(
            src_ref=q_ref.at[cc],
            dst_ref=qbuf.at[y, from_z, from_c],
            send_sem=qz_send.at[zz, cc],
            recv_sem=qz_recv.at[from_z, from_c],
            device_id=device(zz, y, cc),
            device_id_type=MESH,
        )

    q_copy(z, other, z, c).start()
    for off in range(1, A):
        zz = lax.rem(z + off, A)
        for cc in range(CORES):
            q_copy(zz, cc, z, c).start()
    qbuf[y, z, c] = q_ref[c]

    def kv_copy(index, buf, base):
        return pltpu.make_async_remote_copy(
            src_ref=prompt_hbm.at[
                :, :, pl.ds(pl.multiple_of(base + other * half_width, 128), half_width)
            ],
            dst_ref=buf.at[:, pl.ds(span, span), :],
            send_sem=kv_send.at[index],
            recv_sem=kv_recv.at[index],
            device_id=device(z, y, other),
            device_id_type=MESH,
        )

    kv_copies = [kv_copy(0, kbuf, 0), kv_copy(1, vbuf, kv_width)]
    for copy in kv_copies:
        copy.start()

    def y_copy(zz, yy, from_y):
        return pltpu.make_async_remote_copy(
            src_ref=qbuf.at[y, zz],
            dst_ref=qbuf.at[from_y, zz],
            send_sem=qy_send.at[yy, zz],
            recv_sem=qy_recv.at[from_y, zz],
            device_id=device(z, yy, c),
            device_id_type=MESH,
        )

    def forward(off):
        zz = lax.rem(z - off + A, A)
        if off == 0:
            q_copy(z, other, z, other).wait_recv()
        else:
            for cc in range(CORES):
                q_copy(zz, cc, zz, cc).wait_recv()
        for step in range(1, B):
            yy = lax.rem(y + step, B)
            y_copy(zz, yy, y).start()

    length = sbuf.shape[1]
    position = lax.broadcasted_iota(jnp.int32, (group, length), 1)

    def suffix(cand):
        suffix_copies[cand].wait()
        live = position < BLOCK * blocks_ref[cand]
        for head in range(kv_heads):
            side, inner = head // half_heads, head % half_heads
            start = inner * piece + cand * group
            query = q_ref[side].astype(F32)[start : start + group].astype(BF16)
            keys = sbuf[cand, :, head * HD : (head + 1) * HD]
            values = sbuf[cand, :, kv_width + head * HD : kv_width + (head + 1) * HD]
            logits = (
                lax.dot_general(query, keys, (((1,), (1,)), ((), ())), preferred_element_type=F32)
                * scale
            )
            logits = jnp.where(live, logits, FLOOR)
            top = jnp.max(logits, axis=1, keepdims=True)
            weights = jnp.where(live, jnp.exp(logits - top), 0.0)
            total = jnp.sum(weights, axis=1, keepdims=True)
            suf_mix[side, start : start + group, :] = jnp.dot(
                weights.astype(BF16), values, preferred_element_type=F32
            )
            suf_stat[side, 0, start : start + group, :] = jnp.broadcast_to(top, (group, 128))
            suf_stat[side, 1, start : start + group, :] = jnp.broadcast_to(total, (group, 128))

    forward(0)
    order = list(range(1, A))
    for cand in range(cands):
        suffix(cand)
        if cand < len(order):
            forward(order[cand])
    for off in order[cands:]:
        forward(off)

    for copy in local:
        copy.wait()
    for copy in kv_copies:
        copy.wait()

    def attend(yy, zz):
        packets = [qbuf[yy, zz, cc].astype(F32) for cc in range(CORES)]
        marks = jnp.concatenate(
            [
                jnp.broadcast_to(packets[cc][rows + cand : rows + cand + 1], (group, 128))
                for cc in range(CORES)
                for cand in range(cands)
            ],
            axis=0,
        )
        marks = jnp.concatenate([marks] * (CORES * span // 128), axis=1)
        tops, totals, mixes = [], [], []
        for head in range(half_heads):
            query = jnp.concatenate(
                [packets[cc][head * piece : (head + 1) * piece] for cc in range(CORES)], axis=0
            ).astype(BF16)
            lanes = slice(head * HD, (head + 1) * HD)
            logits = None
            for prompt in range(prompts):
                part = lax.dot_general(
                    query,
                    kbuf[prompt, :, lanes],
                    (((1,), (1,)), ((), ())),
                    preferred_element_type=F32,
                )
                logits = part if prompt == 0 else jnp.where(marks == prompt, part, logits)
            logits = logits * scale
            top = jnp.max(logits, axis=1, keepdims=True)
            weights = jnp.exp(logits - top)
            totals.append(jnp.sum(weights, axis=1, keepdims=True))
            tops.append(top)
            mix = None
            for prompt in range(prompts):
                part = jnp.dot(
                    jnp.where(marks == prompt, weights, 0.0).astype(BF16),
                    vbuf[prompt, :, lanes],
                    preferred_element_type=F32,
                )
                mix = part if mix is None else mix + part
            mixes.append(mix)

        def side(parts, cc):
            return jnp.concatenate([p[cc * piece : (cc + 1) * piece] for p in parts], axis=0)

        stat = to_lanes([side(tops, 0), side(tops, 1), side(totals, 0), side(totals, 1)])
        return stat, [side(mixes, cc) for cc in range(CORES)]

    def own(off, carry):
        zz = lax.rem(z - off + A, A)
        stat, mixes = attend(y, zz)
        own_stat[zz] = stat
        for cc in range(CORES):
            own_mix[zz, cc] = mixes[cc]
        return carry

    lax.fori_loop(0, A, own, 0)

    def ym_copy(zz, yy, from_y):
        return pltpu.make_async_remote_copy(
            src_ref=y_mix.at[yy, zz],
            dst_ref=y_mix_in.at[from_y, zz],
            send_sem=ym_send.at[yy, zz],
            recv_sem=ym_recv.at[from_y, zz],
            device_id=device(z, yy, c),
            device_id_type=MESH,
        )

    def ys_copy(zz, yy, from_y):
        return pltpu.make_async_remote_copy(
            src_ref=y_stat.at[yy, zz],
            dst_ref=y_stat_in.at[from_y, zz],
            send_sem=ys_send.at[yy, zz],
            recv_sem=ys_recv.at[from_y, zz],
            device_id=device(z, yy, c),
            device_id_type=MESH,
        )

    def helped(off, carry):
        zz = lax.rem(z - off + A, A)
        for step in range(1, B):
            yy = lax.rem(y + step, B)
            y_copy(zz, yy, yy).wait_recv()
            stat, mixes = attend(yy, zz)
            y_stat[yy, zz] = stat
            for cc in range(CORES):
                y_mix[yy, zz, cc] = mixes[cc].astype(BF16)
            ym_copy(zz, yy, y).start()
            ys_copy(zz, yy, y).start()
        return carry

    lax.fori_loop(0, A, helped, 0)

    def zm_copy(zz, cc, from_z, from_c):
        return pltpu.make_async_remote_copy(
            src_ref=z_mix.at[zz, cc],
            dst_ref=z_mix_in.at[from_z, from_c],
            send_sem=zm_send.at[zz, cc],
            recv_sem=zm_recv.at[from_z, from_c],
            device_id=device(zz, y, cc),
            device_id_type=MESH,
        )

    def zs_copy(zz, cc, from_z, from_c):
        return pltpu.make_async_remote_copy(
            src_ref=z_stat.at[zz, cc],
            dst_ref=z_stat_in.at[from_z, from_c],
            send_sem=zs_send.at[zz, cc],
            recv_sem=zs_recv.at[from_z, from_c],
            device_id=device(zz, y, cc),
            device_id_type=MESH,
        )

    def merged(zz):
        for step in range(1, B):
            yy = lax.rem(y + step, B)
            ym_copy(zz, yy, yy).wait_recv()
            ys_copy(zz, yy, yy).wait_recv()
        stats = [own_stat[zz]]
        for step in range(1, B):
            stats.append(y_stat_in[lax.rem(y + step, B), zz])
        top = functools.reduce(jnp.maximum, [s[0:2] for s in stats])
        factors = [jnp.exp(s[0:2] - top) for s in stats]
        total = sum(f * s[2:4] for f, s in zip(factors, stats))
        columns = to_columns(jnp.concatenate(factors, axis=0), rows)
        results = []
        for cc in range(CORES):
            mix = own_mix[zz, cc] * columns[:, cc : cc + 1]
            for step in range(1, B):
                arrived = y_mix_in[lax.rem(y + step, B), zz, cc].astype(F32)
                index = step * CORES + cc
                mix = mix + arrived * columns[:, index : index + 1]
            stat = jnp.concatenate(
                [top[cc : cc + 1], total[cc : cc + 1], jnp.zeros((6, 128), F32)], axis=0
            )
            results.append((mix.astype(BF16), stat))
        return results

    def returned(off, carry):
        zz = lax.rem(z - off + A, A)
        for cc, (mix, stat) in enumerate(merged(zz)):
            z_mix[zz, cc] = mix
            z_stat[zz, cc] = stat
            zm_copy(zz, cc, z, c).start()
            zs_copy(zz, cc, z, c).start()
        return carry

    lax.fori_loop(1, A, returned, 0)
    for cc, (mix, stat) in enumerate(merged(z)):
        z_mix[z, cc] = mix
        z_stat[z, cc] = stat
    zm_copy(z, other, z, c).start()
    zs_copy(z, other, z, c).start()
    z_mix_in[z, c] = z_mix[z, c]
    z_stat_in[z, c] = z_stat[z, c]

    zm_copy(z, other, z, other).wait_recv()
    zs_copy(z, other, z, other).wait_recv()
    for off in range(1, A):
        zz = lax.rem(z + off, A)
        for cc in range(CORES):
            zm_copy(zz, cc, zz, cc).wait_recv()
            zs_copy(zz, cc, zz, cc).wait_recv()

    scores = [0.0] * cands
    for side in range(CORES):
        suf = to_lanes([suf_stat[side, 0][:, 0:1], suf_stat[side, 1][:, 0:1]])
        stats = [z_stat_in[zz, side] for zz in range(A)] + [suf]
        top = functools.reduce(jnp.maximum, [s[0:1] for s in stats])
        factors = [jnp.exp(s[0:1] - top) for s in stats]
        total = sum(f * s[1:2] for f, s in zip(factors, stats))
        total = jnp.where(total > 0.0, total, 1.0)
        columns = to_columns(jnp.concatenate([f / total for f in factors], axis=0), rows)
        mix = suf_mix[side] * columns[:, A : A + 1]
        for zz in range(A):
            mix = mix + z_mix_in[zz, side].astype(F32) * columns[:, zz : zz + 1]
        half_rows = half_heads * group
        for cand in range(cands):
            picked = jnp.concatenate(
                [
                    mix[head * piece + cand * group : head * piece + (cand + 1) * group]
                    for head in range(half_heads)
                ],
                axis=0,
            ).astype(BF16)
            out_ref[cand, side * half_rows : (side + 1) * half_rows, :] = picked
            term = picked.astype(F32) * weight_ref[side * half_rows : (side + 1) * half_rows]
            scores[cand] = scores[cand] + jnp.sum(term)
    row = lax.broadcasted_iota(jnp.int32, (8, 128), 0)
    tile = jnp.zeros((8, 128), F32)
    for cand in range(cands):
        tile = jnp.where(row == cand, scores[cand], tile)
    score_ref[...] = tile

    q_copy(z, other, z, c).wait_send()
    zm_copy(z, other, z, c).wait_send()
    zs_copy(z, other, z, c).wait_send()

    def drain_z(off, carry):
        zz = lax.rem(z + off, A)
        for cc in range(CORES):
            q_copy(zz, cc, z, c).wait_send()
            zm_copy(zz, cc, z, c).wait_send()
            zs_copy(zz, cc, z, c).wait_send()
        return carry

    lax.fori_loop(1, A, drain_z, 0)

    def drain_y(zz, carry):
        for step in range(1, B):
            yy = lax.rem(y + step, B)
            y_copy(zz, yy, y).wait_send()
            ym_copy(zz, yy, y).wait_send()
            ys_copy(zz, yy, y).wait_send()
        return carry

    lax.fori_loop(0, A, drain_y, 0)


def body(A, B, queries, prompt_of, suffix_cache, suffix_blocks, prompt_cache, reward_weight):
    cands = queries.shape[0]
    heads = queries.shape[1] // HD
    prompts, span, width = prompt_cache.shape
    kv_heads = width // 2 // HD
    group = heads // kv_heads
    half_heads = kv_heads // CORES
    rows = half_heads * cands * group
    packet = rows + 16
    half_width = half_heads * HD

    dma = pltpu.SemaphoreType.DMA

    attended, scores = pl.pallas_call(
        functools.partial(kernel, (A, B, cands, kv_heads, group)),
        out_shape=(
            jax.ShapeDtypeStruct((cands, heads, HD), BF16),
            jax.ShapeDtypeStruct((8, 128), F32),
        ),
        in_specs=[
            pl.BlockSpec(memory_space=pltpu.HBM),
        ]
        * 6,
        out_specs=(
            pl.BlockSpec(memory_space=pltpu.VMEM),
            pl.BlockSpec(memory_space=pltpu.VMEM),
        ),
        scratch_shapes=[
            pltpu.VMEM(queries.shape, BF16),
            pltpu.VMEM((CORES, packet, HD), BF16),
            pltpu.SMEM((1, cands), jnp.int32),
            pltpu.SMEM(suffix_blocks.shape, jnp.int32),
            pltpu.VMEM((heads, HD), F32),
            dma((4,)),
            pltpu.VMEM((prompts, CORES * span, half_width), BF16),
            pltpu.VMEM((prompts, CORES * span, half_width), BF16),
            pltpu.VMEM(suffix_cache.shape, BF16),
            pltpu.VMEM((B, A, CORES, packet, HD), BF16),
            pltpu.VMEM((A, CORES, rows, HD), F32),
            pltpu.VMEM((A, 8, 128), F32),
            pltpu.VMEM((B, A, CORES, rows, HD), BF16),
            pltpu.VMEM((B, A, 8, 128), F32),
            pltpu.VMEM((B, A, CORES, rows, HD), BF16),
            pltpu.VMEM((B, A, 8, 128), F32),
            pltpu.VMEM((A, CORES, rows, HD), BF16),
            pltpu.VMEM((A, CORES, 8, 128), F32),
            pltpu.VMEM((A, CORES, rows, HD), BF16),
            pltpu.VMEM((A, CORES, 8, 128), F32),
            pltpu.VMEM((CORES, rows, HD), F32),
            pltpu.VMEM((CORES, 2, rows, 128), F32),
            dma((2,)),
            dma((2,)),
            dma((2,)),
            dma((cands,)),
            dma((A, CORES)),
            dma((A, CORES)),
            dma((B, A)),
            dma((B, A)),
            dma((B, A)),
            dma((B, A)),
            dma((B, A)),
            dma((B, A)),
            dma((A, CORES)),
            dma((A, CORES)),
            dma((A, CORES)),
            dma((A, CORES)),
        ],
        compiler_params=pltpu.CompilerParams(
            collective_id=0, has_side_effects=True, vmem_limit_bytes=63 * 1024 * 1024
        ),
    )(
        queries,
        prompt_of.reshape(1, cands),
        suffix_blocks,
        reward_weight.reshape(heads, HD),
        prompt_cache,
        suffix_cache,
    )
    return attended.reshape(cands, heads * HD), scores[:cands, 0]


def solution(mesh):
    chips = mesh.shape["seq"] // CORES
    B = 1
    while B * B * 4 <= chips and chips % (B * 2) == 0:
        B *= 2
    A = chips // B
    placed = (
        P(("groups", "seq"), None),
        P(("groups", "seq"), None),
        P(("groups", "seq"), None, None),
        P(("groups", "seq")),
        P("groups", "seq", None),
        P(),
    )
    return jax.shard_map(
        functools.partial(body, A, B),
        mesh=mesh,
        in_specs=placed,
        out_specs=(P(("groups", "seq"), None), P(("groups", "seq"))),
        check_vma=False,
    )
```

```python
import functools
import math

import jax
import jax.numpy as jnp
from jax import lax
from jax.experimental import pallas as pl
from jax.experimental.pallas import tpu as pltpu
from jax.sharding import PartitionSpec as P

HD = 128
BLOCK = 128
CORES = 2
FLOOR = -1e30
MESH = pl.DeviceIdType.MESH
F32 = jnp.float32
BF16 = jnp.bfloat16


def to_lanes(columns):
    rows = columns[0].shape[0]
    lane = lax.broadcasted_iota(jnp.int32, (rows, 128), 1)
    tile = jnp.zeros((rows, 128), F32)
    for index, column in enumerate(columns):
        tile = jnp.where(lane == index, column, tile)
    if rows < 128:
        tile = jnp.concatenate([tile, jnp.zeros((128 - rows, 128), F32)], axis=0)
    return jnp.transpose(tile)[:8]


def to_columns(lanes, rows):
    count = lanes.shape[0]
    tile = jnp.concatenate([lanes, jnp.zeros((128 - count, 128), F32)], axis=0)
    return jnp.transpose(tile)[:rows]


def kernel(
    sizes,
    q_hbm,
    ids_hbm,
    blocks_hbm,
    weight_hbm,
    prompt_hbm,
    suffix_hbm,
    out_ref,
    score_ref,
    q_raw,
    q_ref,
    ids_ref,
    blocks_ref,
    weight_ref,
    small_sem,
    kbuf,
    vbuf,
    sbuf,
    qbuf,
    own_mix,
    own_stat,
    y_mix,
    y_stat,
    y_mix_in,
    y_stat_in,
    z_mix,
    z_stat,
    z_mix_in,
    z_stat_in,
    suf_mix,
    suf_stat,
    kv_local,
    kv_send,
    kv_recv,
    suf_sem,
    qz_send,
    qz_recv,
    qy_send,
    qy_recv,
    ym_send,
    ym_recv,
    ys_send,
    ys_recv,
    zm_send,
    zm_recv,
    zs_send,
    zs_recv,
):
    A, B, cands, kv_heads, group = sizes
    half_heads = kv_heads // CORES
    piece = cands * group
    rows = half_heads * piece
    half_width = half_heads * HD
    kv_width = kv_heads * HD
    span = prompt_hbm.shape[1]
    prompts = prompt_hbm.shape[0]
    scale = HD**-0.5

    me = lax.axis_index("seq")
    c = lax.rem(me, CORES)
    y = lax.rem(me // CORES, B)
    z = me // (CORES * B)
    other = 1 - c

    def device(zz, yy, cc):
        return {"seq": (zz * B + yy) * CORES + cc}

    small = []
    for index, (src, dst) in enumerate(
        (
            (q_hbm, q_raw),
            (ids_hbm, ids_ref),
            (blocks_hbm, blocks_ref),
            (weight_hbm, weight_ref),
        )
    ):
        copy = pltpu.make_async_copy(src, dst, small_sem.at[index])
        copy.start()
        small.append(copy)
    local = []
    for index, (buf, base) in enumerate(((kbuf, 0), (vbuf, kv_width))):
        copy = pltpu.make_async_copy(
            prompt_hbm.at[:, :, pl.ds(pl.multiple_of(base + c * half_width, 128), half_width)],
            buf.at[:, pl.ds(0, span), :],
            kv_local.at[index],
        )
        copy.start()
        local.append(copy)
    suffix_copies = []
    for cand in range(cands):
        copy = pltpu.make_async_copy(suffix_hbm.at[cand], sbuf.at[cand], suf_sem.at[cand])
        copy.start()
        suffix_copies.append(copy)

    barrier = pltpu.get_barrier_semaphore()
    pl.semaphore_signal(barrier, inc=1, device_id=device(z, y, other), device_id_type=MESH)
    for off in range(1, A):
        zz = lax.rem(z + off, A)
        for cc in range(CORES):
            pl.semaphore_signal(barrier, inc=1, device_id=device(zz, y, cc), device_id_type=MESH)
    for off in range(1, B):
        yy = lax.rem(y + off, B)
        pl.semaphore_signal(barrier, inc=1, device_id=device(z, yy, c), device_id_type=MESH)

    small[0].wait()
    small[1].wait()
    raw = q_raw[...].astype(F32)
    by_head = [raw[cand : cand + 1].reshape(kv_heads * group, HD) for cand in range(cands)]
    row = lax.broadcasted_iota(jnp.int32, (16, HD), 0)
    marked = jnp.zeros((16, HD), F32)
    for cand in range(cands):
        marked = jnp.where(row == cand, ids_ref[0, cand].astype(F32), marked)
    for side in range(CORES):
        pieces = [
            by_head[cand][(side * half_heads + head) * group :][:group]
            for head in range(half_heads)
            for cand in range(cands)
        ]
        q_ref[side] = jnp.concatenate(pieces + [marked], axis=0).astype(BF16)
    small[2].wait()
    small[3].wait()
    pl.semaphore_wait(barrier, 1 + CORES * (A - 1) + (B - 1))

    def q_copy(zz, cc, from_z, from_c):
        return pltpu.make_async_remote_copy(
            src_ref=q_ref.at[cc],
            dst_ref=qbuf.at[y, from_z, from_c],
            send_sem=qz_send.at[zz, cc],
            recv_sem=qz_recv.at[from_z, from_c],
            device_id=device(zz, y, cc),
            device_id_type=MESH,
        )

    q_copy(z, other, z, c).start()
    for off in range(1, A):
        zz = lax.rem(z + off, A)
        for cc in range(CORES):
            q_copy(zz, cc, z, c).start()
    qbuf[y, z, c] = q_ref[c]

    def kv_copy(index, buf, base):
        return pltpu.make_async_remote_copy(
            src_ref=prompt_hbm.at[
                :, :, pl.ds(pl.multiple_of(base + other * half_width, 128), half_width)
            ],
            dst_ref=buf.at[:, pl.ds(span, span), :],
            send_sem=kv_send.at[index],
            recv_sem=kv_recv.at[index],
            device_id=device(z, y, other),
            device_id_type=MESH,
        )

    kv_copies = [kv_copy(0, kbuf, 0), kv_copy(1, vbuf, kv_width)]
    for copy in kv_copies:
        copy.start()

    def y_copy(zz, yy, from_y):
        return pltpu.make_async_remote_copy(
            src_ref=qbuf.at[y, zz],
            dst_ref=qbuf.at[from_y, zz],
            send_sem=qy_send.at[yy, zz],
            recv_sem=qy_recv.at[from_y, zz],
            device_id=device(z, yy, c),
            device_id_type=MESH,
        )

    def forward(off):
        zz = lax.rem(z - off + A, A)
        if off == 0:
            q_copy(z, other, z, other).wait_recv()
        else:
            for cc in range(CORES):
                q_copy(zz, cc, zz, cc).wait_recv()
        for step in range(1, B):
            yy = lax.rem(y + step, B)
            y_copy(zz, yy, y).start()

    length = sbuf.shape[1]
    position = lax.broadcasted_iota(jnp.int32, (group, length), 1)

    def suffix(cand):
        suffix_copies[cand].wait()
        live = position < BLOCK * blocks_ref[cand]
        for head in range(kv_heads):
            side, inner = head // half_heads, head % half_heads
            start = inner * piece + cand * group
            query = q_ref[side].astype(F32)[start : start + group].astype(BF16)
            keys = sbuf[cand, :, head * HD : (head + 1) * HD]
            values = sbuf[cand, :, kv_width + head * HD : kv_width + (head + 1) * HD]
            logits = (
                lax.dot_general(query, keys, (((1,), (1,)), ((), ())), preferred_element_type=F32)
                * scale
            )
            logits = jnp.where(live, logits, FLOOR)
            top = jnp.max(logits, axis=1, keepdims=True)
            weights = jnp.where(live, jnp.exp(logits - top), 0.0)
            total = jnp.sum(weights, axis=1, keepdims=True)
            suf_mix[side, start : start + group, :] = jnp.dot(
                weights.astype(BF16), values, preferred_element_type=F32
            )
            suf_stat[side, 0, start : start + group, :] = jnp.broadcast_to(top, (group, 128))
            suf_stat[side, 1, start : start + group, :] = jnp.broadcast_to(total, (group, 128))

    forward(0)
    order = list(range(1, A))
    for cand in range(cands):
        suffix(cand)
        if cand < len(order):
            forward(order[cand])
    for off in order[cands:]:
        forward(off)

    suf_lanes = [
        to_lanes([suf_stat[side, 0][:, 0:1], suf_stat[side, 1][:, 0:1]]) for side in range(CORES)
    ]
    for copy in local:
        copy.wait()
    for copy in kv_copies:
        copy.wait()

    def attend(yy, zz):
        packets = [qbuf[yy, zz, cc].astype(F32) for cc in range(CORES)]
        marks = jnp.concatenate(
            [
                jnp.broadcast_to(packets[cc][rows + cand : rows + cand + 1], (group, 128))
                for cc in range(CORES)
                for cand in range(cands)
            ],
            axis=0,
        )
        marks = jnp.concatenate([marks] * (CORES * span // 128), axis=1)
        tops, totals, mixes = [], [], []
        for head in range(half_heads):
            query = jnp.concatenate(
                [packets[cc][head * piece : (head + 1) * piece] for cc in range(CORES)], axis=0
            ).astype(BF16)
            lanes = slice(head * HD, (head + 1) * HD)
            logits = None
            for prompt in range(prompts):
                part = lax.dot_general(
                    query,
                    kbuf[prompt, :, lanes],
                    (((1,), (1,)), ((), ())),
                    preferred_element_type=F32,
                )
                logits = part if prompt == 0 else jnp.where(marks == prompt, part, logits)
            logits = logits * scale
            top = jnp.max(logits, axis=1, keepdims=True)
            weights = jnp.exp(logits - top)
            totals.append(jnp.sum(weights, axis=1, keepdims=True))
            tops.append(top)
            mix = None
            for prompt in range(prompts):
                part = jnp.dot(
                    jnp.where(marks == prompt, weights, 0.0).astype(BF16),
                    vbuf[prompt, :, lanes],
                    preferred_element_type=F32,
                )
                mix = part if mix is None else mix + part
            mixes.append(mix)

        def side(parts, cc):
            return jnp.concatenate([p[cc * piece : (cc + 1) * piece] for p in parts], axis=0)

        stat = to_lanes([side(tops, 0), side(tops, 1), side(totals, 0), side(totals, 1)])
        return stat, [side(mixes, cc) for cc in range(CORES)]

    def own(off):
        zz = lax.rem(z - off + A, A)
        stat, mixes = attend(y, zz)
        own_stat[zz] = stat
        for cc in range(CORES):
            own_mix[zz, cc] = mixes[cc]

    def ym_copy(zz, yy, from_y):
        return pltpu.make_async_remote_copy(
            src_ref=y_mix.at[yy, zz],
            dst_ref=y_mix_in.at[from_y, zz],
            send_sem=ym_send.at[yy, zz],
            recv_sem=ym_recv.at[from_y, zz],
            device_id=device(z, yy, c),
            device_id_type=MESH,
        )

    def ys_copy(zz, yy, from_y):
        return pltpu.make_async_remote_copy(
            src_ref=y_stat.at[yy, zz],
            dst_ref=y_stat_in.at[from_y, zz],
            send_sem=ys_send.at[yy, zz],
            recv_sem=ys_recv.at[from_y, zz],
            device_id=device(z, yy, c),
            device_id_type=MESH,
        )

    def helped(off):
        zz = lax.rem(z - off + A, A)
        for step in range(1, B):
            yy = lax.rem(y + step, B)
            y_copy(zz, yy, yy).wait_recv()
            stat, mixes = attend(yy, zz)
            y_stat[yy, zz] = stat
            for cc in range(CORES):
                y_mix[yy, zz, cc] = mixes[cc].astype(BF16)
            ym_copy(zz, yy, y).start()
            ys_copy(zz, yy, y).start()

    def zm_copy(zz, cc, from_z, from_c):
        return pltpu.make_async_remote_copy(
            src_ref=z_mix.at[zz, cc],
            dst_ref=z_mix_in.at[from_z, from_c],
            send_sem=zm_send.at[zz, cc],
            recv_sem=zm_recv.at[from_z, from_c],
            device_id=device(zz, y, cc),
            device_id_type=MESH,
        )

    def zs_copy(zz, cc, from_z, from_c):
        return pltpu.make_async_remote_copy(
            src_ref=z_stat.at[zz, cc],
            dst_ref=z_stat_in.at[from_z, from_c],
            send_sem=zs_send.at[zz, cc],
            recv_sem=zs_recv.at[from_z, from_c],
            device_id=device(zz, y, cc),
            device_id_type=MESH,
        )

    def merged(zz):
        for step in range(1, B):
            yy = lax.rem(y + step, B)
            ym_copy(zz, yy, yy).wait_recv()
            ys_copy(zz, yy, yy).wait_recv()
        stats = [own_stat[zz]]
        for step in range(1, B):
            stats.append(y_stat_in[lax.rem(y + step, B), zz])
        top = functools.reduce(jnp.maximum, [s[0:2] for s in stats])
        factors = [jnp.exp(s[0:2] - top) for s in stats]
        total = sum(f * s[2:4] for f, s in zip(factors, stats))
        columns = to_columns(jnp.concatenate(factors, axis=0), rows)
        results = []
        for cc in range(CORES):
            mix = own_mix[zz, cc] * columns[:, cc : cc + 1]
            for step in range(1, B):
                arrived = y_mix_in[lax.rem(y + step, B), zz, cc].astype(F32)
                index = step * CORES + cc
                mix = mix + arrived * columns[:, index : index + 1]
            stat = jnp.concatenate(
                [top[cc : cc + 1], total[cc : cc + 1], jnp.zeros((6, 128), F32)], axis=0
            )
            results.append((mix.astype(BF16), stat))
        return results

    def returned(off):
        zz = lax.rem(z - off + A, A)
        for cc, (mix, stat) in enumerate(merged(zz)):
            z_mix[zz, cc] = mix
            z_stat[zz, cc] = stat
            zm_copy(zz, cc, z, c).start()
            zs_copy(zz, cc, z, c).start()

    helped(0)
    for off in range(1, A):
        own(off)
        helped(off)
        if off >= 2:
            returned(off - 1)
    own(0)
    returned(A - 1)
    for cc, (mix, stat) in enumerate(merged(z)):
        z_mix[z, cc] = mix
        z_stat[z, cc] = stat
    zm_copy(z, other, z, c).start()
    zs_copy(z, other, z, c).start()
    z_mix_in[z, c] = z_mix[z, c]
    z_stat_in[z, c] = z_stat[z, c]

    zm_copy(z, other, z, other).wait_recv()
    zs_copy(z, other, z, other).wait_recv()
    for off in range(1, A):
        zz = lax.rem(z + off, A)
        for cc in range(CORES):
            zm_copy(zz, cc, zz, cc).wait_recv()
            zs_copy(zz, cc, zz, cc).wait_recv()

    scores = [0.0] * cands
    for side in range(CORES):
        stats = [z_stat_in[zz, side] for zz in range(A)] + [suf_lanes[side]]
        top = functools.reduce(jnp.maximum, [s[0:1] for s in stats])
        factors = [jnp.exp(s[0:1] - top) for s in stats]
        total = sum(f * s[1:2] for f, s in zip(factors, stats))
        total = jnp.where(total > 0.0, total, 1.0)
        columns = to_columns(jnp.concatenate([f / total for f in factors], axis=0), rows)
        mix = suf_mix[side] * columns[:, A : A + 1]
        for zz in range(A):
            mix = mix + z_mix_in[zz, side].astype(F32) * columns[:, zz : zz + 1]
        half_rows = half_heads * group
        for cand in range(cands):
            picked = jnp.concatenate(
                [
                    mix[head * piece + cand * group : head * piece + (cand + 1) * group]
                    for head in range(half_heads)
                ],
                axis=0,
            ).astype(BF16)
            out_ref[cand, side * half_rows : (side + 1) * half_rows, :] = picked
            term = picked.astype(F32) * weight_ref[side * half_rows : (side + 1) * half_rows]
            scores[cand] = scores[cand] + jnp.sum(term)
    row = lax.broadcasted_iota(jnp.int32, (8, 128), 0)
    tile = jnp.zeros((8, 128), F32)
    for cand in range(cands):
        tile = jnp.where(row == cand, scores[cand], tile)
    score_ref[...] = tile

    q_copy(z, other, z, c).wait_send()
    zm_copy(z, other, z, c).wait_send()
    zs_copy(z, other, z, c).wait_send()

    def drain_z(off, carry):
        zz = lax.rem(z + off, A)
        for cc in range(CORES):
            q_copy(zz, cc, z, c).wait_send()
            zm_copy(zz, cc, z, c).wait_send()
            zs_copy(zz, cc, z, c).wait_send()
        return carry

    lax.fori_loop(1, A, drain_z, 0)

    def drain_y(zz, carry):
        for step in range(1, B):
            yy = lax.rem(y + step, B)
            y_copy(zz, yy, y).wait_send()
            ym_copy(zz, yy, y).wait_send()
            ys_copy(zz, yy, y).wait_send()
        return carry

    lax.fori_loop(0, A, drain_y, 0)


def body(A, B, queries, prompt_of, suffix_cache, suffix_blocks, prompt_cache, reward_weight):
    cands = queries.shape[0]
    heads = queries.shape[1] // HD
    prompts, span, width = prompt_cache.shape
    kv_heads = width // 2 // HD
    group = heads // kv_heads
    half_heads = kv_heads // CORES
    rows = half_heads * cands * group
    packet = rows + 16
    half_width = half_heads * HD

    dma = pltpu.SemaphoreType.DMA

    attended, scores = pl.pallas_call(
        functools.partial(kernel, (A, B, cands, kv_heads, group)),
        out_shape=(
            jax.ShapeDtypeStruct((cands, heads, HD), BF16),
            jax.ShapeDtypeStruct((8, 128), F32),
        ),
        in_specs=[
            pl.BlockSpec(memory_space=pltpu.HBM),
        ]
        * 6,
        out_specs=(
            pl.BlockSpec(memory_space=pltpu.VMEM),
            pl.BlockSpec(memory_space=pltpu.VMEM),
        ),
        scratch_shapes=[
            pltpu.VMEM(queries.shape, BF16),
            pltpu.VMEM((CORES, packet, HD), BF16),
            pltpu.SMEM((1, cands), jnp.int32),
            pltpu.SMEM(suffix_blocks.shape, jnp.int32),
            pltpu.VMEM((heads, HD), F32),
            dma((4,)),
            pltpu.VMEM((prompts, CORES * span, half_width), BF16),
            pltpu.VMEM((prompts, CORES * span, half_width), BF16),
            pltpu.VMEM(suffix_cache.shape, BF16),
            pltpu.VMEM((B, A, CORES, packet, HD), BF16),
            pltpu.VMEM((A, CORES, rows, HD), F32),
            pltpu.VMEM((A, 8, 128), F32),
            pltpu.VMEM((B, A, CORES, rows, HD), BF16),
            pltpu.VMEM((B, A, 8, 128), F32),
            pltpu.VMEM((B, A, CORES, rows, HD), BF16),
            pltpu.VMEM((B, A, 8, 128), F32),
            pltpu.VMEM((A, CORES, rows, HD), BF16),
            pltpu.VMEM((A, CORES, 8, 128), F32),
            pltpu.VMEM((A, CORES, rows, HD), BF16),
            pltpu.VMEM((A, CORES, 8, 128), F32),
            pltpu.VMEM((CORES, rows, HD), F32),
            pltpu.VMEM((CORES, 2, rows, 128), F32),
            dma((2,)),
            dma((2,)),
            dma((2,)),
            dma((cands,)),
            dma((A, CORES)),
            dma((A, CORES)),
            dma((B, A)),
            dma((B, A)),
            dma((B, A)),
            dma((B, A)),
            dma((B, A)),
            dma((B, A)),
            dma((A, CORES)),
            dma((A, CORES)),
            dma((A, CORES)),
            dma((A, CORES)),
        ],
        compiler_params=pltpu.CompilerParams(
            collective_id=0, has_side_effects=True, vmem_limit_bytes=63 * 1024 * 1024
        ),
    )(
        queries,
        prompt_of.reshape(1, cands),
        suffix_blocks,
        reward_weight.reshape(heads, HD),
        prompt_cache,
        suffix_cache,
    )
    return attended.reshape(cands, heads * HD), scores[:cands, 0]


def solution(mesh):
    chips = mesh.shape["seq"] // CORES
    B = 1
    while B * B * 4 <= chips and chips % (B * 2) == 0:
        B *= 2
    A = chips // B
    placed = (
        P(("groups", "seq"), None),
        P(("groups", "seq"), None),
        P(("groups", "seq"), None, None),
        P(("groups", "seq")),
        P("groups", "seq", None),
        P(),
    )
    return jax.shard_map(
        functools.partial(body, A, B),
        mesh=mesh,
        in_specs=placed,
        out_specs=(P(("groups", "seq"), None), P(("groups", "seq"))),
        check_vma=False,
    )
```

```python
import functools
import math

import jax
import jax.numpy as jnp
from jax import lax
from jax.experimental import pallas as pl
from jax.experimental.pallas import tpu as pltpu
from jax.sharding import PartitionSpec as P

HD = 128
BLOCK = 128
CORES = 2
FLOOR = -1e30
MESH = pl.DeviceIdType.MESH
F32 = jnp.float32
BF16 = jnp.bfloat16


def to_lanes(columns):
    rows = columns[0].shape[0]
    lane = lax.broadcasted_iota(jnp.int32, (rows, 128), 1)
    tile = jnp.zeros((rows, 128), F32)
    for index, column in enumerate(columns):
        tile = jnp.where(lane == index, column, tile)
    if rows < 128:
        tile = jnp.concatenate([tile, jnp.zeros((128 - rows, 128), F32)], axis=0)
    return jnp.transpose(tile)[:8]


def to_columns(lanes, rows):
    count = lanes.shape[0]
    tile = jnp.concatenate([lanes, jnp.zeros((128 - count, 128), F32)], axis=0)
    return jnp.transpose(tile)[:rows]


def kernel(
    sizes,
    q_hbm,
    ids_hbm,
    blocks_hbm,
    weight_hbm,
    prompt_hbm,
    suffix_hbm,
    out_ref,
    score_ref,
    q_raw,
    q_ref,
    ids_ref,
    blocks_ref,
    weight_ref,
    small_sem,
    kbuf,
    vbuf,
    sbuf,
    qbuf,
    own_mix,
    own_stat,
    y_mix,
    y_stat,
    y_mix_in,
    y_stat_in,
    z_mix,
    z_stat,
    z_mix_in,
    z_stat_in,
    suf_mix,
    suf_stat,
    kv_local,
    kv_send,
    kv_recv,
    suf_sem,
    qz_send,
    qz_recv,
    qy_send,
    qy_recv,
    ym_send,
    ym_recv,
    ys_send,
    ys_recv,
    zm_send,
    zm_recv,
    zs_send,
    zs_recv,
):
    A, B, cands, kv_heads, group = sizes
    half_heads = kv_heads // CORES
    piece = cands * group
    rows = half_heads * piece
    half_width = half_heads * HD
    kv_width = kv_heads * HD
    span = prompt_hbm.shape[1]
    prompts = prompt_hbm.shape[0]
    scale = HD**-0.5

    me = lax.axis_index("seq")
    c = lax.rem(me, CORES)
    y = lax.rem(me // CORES, B)
    z = me // (CORES * B)
    other = 1 - c

    def device(zz, yy, cc):
        return {"seq": (zz * B + yy) * CORES + cc}

    small = []
    for index, (src, dst) in enumerate(
        (
            (q_hbm, q_raw),
            (ids_hbm, ids_ref),
            (blocks_hbm, blocks_ref),
            (weight_hbm, weight_ref),
        )
    ):
        copy = pltpu.make_async_copy(src, dst, small_sem.at[index])
        copy.start()
        small.append(copy)
    local = []
    for index, (buf, base) in enumerate(((kbuf, 0), (vbuf, kv_width))):
        copy = pltpu.make_async_copy(
            prompt_hbm.at[:, :, pl.ds(pl.multiple_of(base + c * half_width, 128), half_width)],
            buf.at[:, pl.ds(0, span), :],
            kv_local.at[index],
        )
        copy.start()
        local.append(copy)
    suffix_copies = []
    for cand in range(cands):
        copy = pltpu.make_async_copy(suffix_hbm.at[cand], sbuf.at[cand], suf_sem.at[cand])
        copy.start()
        suffix_copies.append(copy)

    barrier = pltpu.get_barrier_semaphore()
    pl.semaphore_signal(barrier, inc=1, device_id=device(z, y, other), device_id_type=MESH)
    for off in range(1, A):
        zz = lax.rem(z + off, A)
        for cc in range(CORES):
            pl.semaphore_signal(barrier, inc=1, device_id=device(zz, y, cc), device_id_type=MESH)
    for off in range(1, B):
        yy = lax.rem(y + off, B)
        pl.semaphore_signal(barrier, inc=1, device_id=device(z, yy, c), device_id_type=MESH)

    small[0].wait()
    small[1].wait()
    raw = q_raw[...].astype(F32)
    by_head = [raw[cand : cand + 1].reshape(kv_heads * group, HD) for cand in range(cands)]
    row = lax.broadcasted_iota(jnp.int32, (16, HD), 0)
    marked = jnp.zeros((16, HD), F32)
    for cand in range(cands):
        marked = jnp.where(row == cand, ids_ref[0, cand].astype(F32), marked)
    for side in range(CORES):
        pieces = [
            by_head[cand][(side * half_heads + head) * group :][:group]
            for head in range(half_heads)
            for cand in range(cands)
        ]
        q_ref[side] = jnp.concatenate(pieces + [marked], axis=0).astype(BF16)
    small[2].wait()
    small[3].wait()
    pl.semaphore_wait(barrier, 1 + CORES * (A - 1) + (B - 1))

    def q_copy(zz, cc, from_z, from_c):
        return pltpu.make_async_remote_copy(
            src_ref=q_ref.at[cc],
            dst_ref=qbuf.at[y, from_z, from_c],
            send_sem=qz_send.at[zz, cc],
            recv_sem=qz_recv.at[from_z, from_c],
            device_id=device(zz, y, cc),
            device_id_type=MESH,
        )

    q_copy(z, other, z, c).start()
    for off in range(1, A):
        zz = lax.rem(z + off, A)
        for cc in range(CORES):
            q_copy(zz, cc, z, c).start()
    qbuf[y, z, c] = q_ref[c]

    def kv_copy(index, buf, base):
        return pltpu.make_async_remote_copy(
            src_ref=prompt_hbm.at[
                :, :, pl.ds(pl.multiple_of(base + other * half_width, 128), half_width)
            ],
            dst_ref=buf.at[:, pl.ds(span, span), :],
            send_sem=kv_send.at[index],
            recv_sem=kv_recv.at[index],
            device_id=device(z, y, other),
            device_id_type=MESH,
        )

    kv_copies = [kv_copy(0, kbuf, 0), kv_copy(1, vbuf, kv_width)]
    for copy in kv_copies:
        copy.start()

    def y_copy(zz, yy, from_y):
        return pltpu.make_async_remote_copy(
            src_ref=qbuf.at[y, zz],
            dst_ref=qbuf.at[from_y, zz],
            send_sem=qy_send.at[yy, zz],
            recv_sem=qy_recv.at[from_y, zz],
            device_id=device(z, yy, c),
            device_id_type=MESH,
        )

    def forward(off):
        zz = lax.rem(z - off + A, A)
        if off == 0:
            q_copy(z, other, z, other).wait_recv()
        else:
            for cc in range(CORES):
                q_copy(zz, cc, zz, cc).wait_recv()
        for step in range(1, B):
            yy = lax.rem(y + step, B)
            y_copy(zz, yy, y).start()

    length = sbuf.shape[1]
    position = lax.broadcasted_iota(jnp.int32, (group, length), 1)

    def suffix(cand):
        suffix_copies[cand].wait()
        live = position < BLOCK * blocks_ref[cand]
        for head in range(kv_heads):
            side, inner = head // half_heads, head % half_heads
            start = inner * piece + cand * group
            query = q_ref[side].astype(F32)[start : start + group].astype(BF16)
            keys = sbuf[cand, :, head * HD : (head + 1) * HD]
            values = sbuf[cand, :, kv_width + head * HD : kv_width + (head + 1) * HD]
            logits = (
                lax.dot_general(query, keys, (((1,), (1,)), ((), ())), preferred_element_type=F32)
                * scale
            )
            logits = jnp.where(live, logits, FLOOR)
            top = jnp.max(logits, axis=1, keepdims=True)
            weights = jnp.where(live, jnp.exp(logits - top), 0.0)
            total = jnp.sum(weights, axis=1, keepdims=True)
            suf_mix[side, start : start + group, :] = jnp.dot(
                weights.astype(BF16), values, preferred_element_type=F32
            )
            suf_stat[side, 0, start : start + group, :] = jnp.broadcast_to(top, (group, 128))
            suf_stat[side, 1, start : start + group, :] = jnp.broadcast_to(total, (group, 128))

    forward(0)
    order = list(range(1, A - 1))
    for cand in range(cands):
        suffix(cand)
        if cand < len(order):
            forward(order[cand])
    for off in order[cands:]:
        forward(off)

    suf_lanes = [
        to_lanes([suf_stat[side, 0][:, 0:1], suf_stat[side, 1][:, 0:1]]) for side in range(CORES)
    ]
    for copy in local:
        copy.wait()
    for copy in kv_copies:
        copy.wait()

    def attend(yy, zz):
        packets = [qbuf[yy, zz, cc].astype(F32) for cc in range(CORES)]
        marks = jnp.concatenate(
            [
                jnp.broadcast_to(packets[cc][rows + cand : rows + cand + 1], (group, 128))
                for cc in range(CORES)
                for cand in range(cands)
            ],
            axis=0,
        )
        marks = jnp.concatenate([marks] * (CORES * span // 128), axis=1)
        tops, totals, mixes = [], [], []
        for head in range(half_heads):
            query = jnp.concatenate(
                [packets[cc][head * piece : (head + 1) * piece] for cc in range(CORES)], axis=0
            ).astype(BF16)
            lanes = slice(head * HD, (head + 1) * HD)
            logits = None
            for prompt in range(prompts):
                part = lax.dot_general(
                    query,
                    kbuf[prompt, :, lanes],
                    (((1,), (1,)), ((), ())),
                    preferred_element_type=F32,
                )
                logits = part if prompt == 0 else jnp.where(marks == prompt, part, logits)
            logits = logits * scale
            top = jnp.max(logits, axis=1, keepdims=True)
            weights = jnp.exp(logits - top)
            totals.append(jnp.sum(weights, axis=1, keepdims=True))
            tops.append(top)
            mix = None
            for prompt in range(prompts):
                part = jnp.dot(
                    jnp.where(marks == prompt, weights, 0.0).astype(BF16),
                    vbuf[prompt, :, lanes],
                    preferred_element_type=F32,
                )
                mix = part if mix is None else mix + part
            mixes.append(mix)

        def side(parts, cc):
            return jnp.concatenate([p[cc * piece : (cc + 1) * piece] for p in parts], axis=0)

        stat = to_lanes([side(tops, 0), side(tops, 1), side(totals, 0), side(totals, 1)])
        return stat, [side(mixes, cc) for cc in range(CORES)]

    def own(off):
        zz = lax.rem(z - off + A, A)
        stat, mixes = attend(y, zz)
        own_stat[zz] = stat
        for cc in range(CORES):
            own_mix[zz, cc] = mixes[cc]

    def ym_copy(zz, yy, from_y):
        return pltpu.make_async_remote_copy(
            src_ref=y_mix.at[yy, zz],
            dst_ref=y_mix_in.at[from_y, zz],
            send_sem=ym_send.at[yy, zz],
            recv_sem=ym_recv.at[from_y, zz],
            device_id=device(z, yy, c),
            device_id_type=MESH,
        )

    def ys_copy(zz, yy, from_y):
        return pltpu.make_async_remote_copy(
            src_ref=y_stat.at[yy, zz],
            dst_ref=y_stat_in.at[from_y, zz],
            send_sem=ys_send.at[yy, zz],
            recv_sem=ys_recv.at[from_y, zz],
            device_id=device(z, yy, c),
            device_id_type=MESH,
        )

    def helped(off):
        zz = lax.rem(z - off + A, A)
        for step in range(1, B):
            yy = lax.rem(y + step, B)
            y_copy(zz, yy, yy).wait_recv()
            stat, mixes = attend(yy, zz)
            y_stat[yy, zz] = stat
            for cc in range(CORES):
                y_mix[yy, zz, cc] = mixes[cc].astype(BF16)
            ym_copy(zz, yy, y).start()
            ys_copy(zz, yy, y).start()

    def zm_copy(zz, cc, from_z, from_c):
        return pltpu.make_async_remote_copy(
            src_ref=z_mix.at[zz, cc],
            dst_ref=z_mix_in.at[from_z, from_c],
            send_sem=zm_send.at[zz, cc],
            recv_sem=zm_recv.at[from_z, from_c],
            device_id=device(zz, y, cc),
            device_id_type=MESH,
        )

    def zs_copy(zz, cc, from_z, from_c):
        return pltpu.make_async_remote_copy(
            src_ref=z_stat.at[zz, cc],
            dst_ref=z_stat_in.at[from_z, from_c],
            send_sem=zs_send.at[zz, cc],
            recv_sem=zs_recv.at[from_z, from_c],
            device_id=device(zz, y, cc),
            device_id_type=MESH,
        )

    def merged(zz):
        for step in range(1, B):
            yy = lax.rem(y + step, B)
            ym_copy(zz, yy, yy).wait_recv()
            ys_copy(zz, yy, yy).wait_recv()
        stats = [own_stat[zz]]
        for step in range(1, B):
            stats.append(y_stat_in[lax.rem(y + step, B), zz])
        top = functools.reduce(jnp.maximum, [s[0:2] for s in stats])
        factors = [jnp.exp(s[0:2] - top) for s in stats]
        total = sum(f * s[2:4] for f, s in zip(factors, stats))
        columns = to_columns(jnp.concatenate(factors, axis=0), rows)
        results = []
        for cc in range(CORES):
            mix = own_mix[zz, cc] * columns[:, cc : cc + 1]
            for step in range(1, B):
                arrived = y_mix_in[lax.rem(y + step, B), zz, cc].astype(F32)
                index = step * CORES + cc
                mix = mix + arrived * columns[:, index : index + 1]
            stat = jnp.concatenate(
                [top[cc : cc + 1], total[cc : cc + 1], jnp.zeros((6, 128), F32)], axis=0
            )
            results.append((mix.astype(BF16), stat))
        return results

    def returned(off):
        zz = lax.rem(z - off + A, A)
        for cc, (mix, stat) in enumerate(merged(zz)):
            z_mix[zz, cc] = mix
            z_stat[zz, cc] = stat
            zm_copy(zz, cc, z, c).start()
            zs_copy(zz, cc, z, c).start()

    helped(0)
    forward(A - 1)
    for off in range(1, A):
        own(off)
        helped(off)
        if off >= 2:
            returned(off - 1)
    own(0)
    returned(A - 1)
    for cc, (mix, stat) in enumerate(merged(z)):
        z_mix[z, cc] = mix
        z_stat[z, cc] = stat
    zm_copy(z, other, z, c).start()
    zs_copy(z, other, z, c).start()
    z_mix_in[z, c] = z_mix[z, c]
    z_stat_in[z, c] = z_stat[z, c]

    zm_copy(z, other, z, other).wait_recv()
    zs_copy(z, other, z, other).wait_recv()
    for off in range(1, A):
        zz = lax.rem(z + off, A)
        for cc in range(CORES):
            zm_copy(zz, cc, zz, cc).wait_recv()
            zs_copy(zz, cc, zz, cc).wait_recv()

    scores = [0.0] * cands
    for side in range(CORES):
        stats = [z_stat_in[zz, side] for zz in range(A)] + [suf_lanes[side]]
        top = functools.reduce(jnp.maximum, [s[0:1] for s in stats])
        factors = [jnp.exp(s[0:1] - top) for s in stats]
        total = sum(f * s[1:2] for f, s in zip(factors, stats))
        total = jnp.where(total > 0.0, total, 1.0)
        columns = to_columns(jnp.concatenate([f / total for f in factors], axis=0), rows)
        mix = suf_mix[side] * columns[:, A : A + 1]
        for zz in range(A):
            mix = mix + z_mix_in[zz, side].astype(F32) * columns[:, zz : zz + 1]
        half_rows = half_heads * group
        for cand in range(cands):
            picked = jnp.concatenate(
                [
                    mix[head * piece + cand * group : head * piece + (cand + 1) * group]
                    for head in range(half_heads)
                ],
                axis=0,
            ).astype(BF16)
            out_ref[cand, side * half_rows : (side + 1) * half_rows, :] = picked
            term = picked.astype(F32) * weight_ref[side * half_rows : (side + 1) * half_rows]
            scores[cand] = scores[cand] + jnp.sum(term)
    row = lax.broadcasted_iota(jnp.int32, (8, 128), 0)
    tile = jnp.zeros((8, 128), F32)
    for cand in range(cands):
        tile = jnp.where(row == cand, scores[cand], tile)
    score_ref[...] = tile

    q_copy(z, other, z, c).wait_send()
    zm_copy(z, other, z, c).wait_send()
    zs_copy(z, other, z, c).wait_send()

    def drain_z(off, carry):
        zz = lax.rem(z + off, A)
        for cc in range(CORES):
            q_copy(zz, cc, z, c).wait_send()
            zm_copy(zz, cc, z, c).wait_send()
            zs_copy(zz, cc, z, c).wait_send()
        return carry

    lax.fori_loop(1, A, drain_z, 0)

    def drain_y(zz, carry):
        for step in range(1, B):
            yy = lax.rem(y + step, B)
            y_copy(zz, yy, y).wait_send()
            ym_copy(zz, yy, y).wait_send()
            ys_copy(zz, yy, y).wait_send()
        return carry

    lax.fori_loop(0, A, drain_y, 0)


def body(A, B, queries, prompt_of, suffix_cache, suffix_blocks, prompt_cache, reward_weight):
    cands = queries.shape[0]
    heads = queries.shape[1] // HD
    prompts, span, width = prompt_cache.shape
    kv_heads = width // 2 // HD
    group = heads // kv_heads
    half_heads = kv_heads // CORES
    rows = half_heads * cands * group
    packet = rows + 16
    half_width = half_heads * HD

    dma = pltpu.SemaphoreType.DMA

    attended, scores = pl.pallas_call(
        functools.partial(kernel, (A, B, cands, kv_heads, group)),
        out_shape=(
            jax.ShapeDtypeStruct((cands, heads, HD), BF16),
            jax.ShapeDtypeStruct((8, 128), F32),
        ),
        in_specs=[
            pl.BlockSpec(memory_space=pltpu.HBM),
        ]
        * 6,
        out_specs=(
            pl.BlockSpec(memory_space=pltpu.VMEM),
            pl.BlockSpec(memory_space=pltpu.VMEM),
        ),
        scratch_shapes=[
            pltpu.VMEM(queries.shape, BF16),
            pltpu.VMEM((CORES, packet, HD), BF16),
            pltpu.SMEM((1, cands), jnp.int32),
            pltpu.SMEM(suffix_blocks.shape, jnp.int32),
            pltpu.VMEM((heads, HD), F32),
            dma((4,)),
            pltpu.VMEM((prompts, CORES * span, half_width), BF16),
            pltpu.VMEM((prompts, CORES * span, half_width), BF16),
            pltpu.VMEM(suffix_cache.shape, BF16),
            pltpu.VMEM((B, A, CORES, packet, HD), BF16),
            pltpu.VMEM((A, CORES, rows, HD), F32),
            pltpu.VMEM((A, 8, 128), F32),
            pltpu.VMEM((B, A, CORES, rows, HD), BF16),
            pltpu.VMEM((B, A, 8, 128), F32),
            pltpu.VMEM((B, A, CORES, rows, HD), BF16),
            pltpu.VMEM((B, A, 8, 128), F32),
            pltpu.VMEM((A, CORES, rows, HD), BF16),
            pltpu.VMEM((A, CORES, 8, 128), F32),
            pltpu.VMEM((A, CORES, rows, HD), BF16),
            pltpu.VMEM((A, CORES, 8, 128), F32),
            pltpu.VMEM((CORES, rows, HD), F32),
            pltpu.VMEM((CORES, 2, rows, 128), F32),
            dma((2,)),
            dma((2,)),
            dma((2,)),
            dma((cands,)),
            dma((A, CORES)),
            dma((A, CORES)),
            dma((B, A)),
            dma((B, A)),
            dma((B, A)),
            dma((B, A)),
            dma((B, A)),
            dma((B, A)),
            dma((A, CORES)),
            dma((A, CORES)),
            dma((A, CORES)),
            dma((A, CORES)),
        ],
        compiler_params=pltpu.CompilerParams(
            collective_id=0, has_side_effects=True, vmem_limit_bytes=63 * 1024 * 1024
        ),
    )(
        queries,
        prompt_of.reshape(1, cands),
        suffix_blocks,
        reward_weight.reshape(heads, HD),
        prompt_cache,
        suffix_cache,
    )
    return attended.reshape(cands, heads * HD), scores[:cands, 0]


def solution(mesh):
    chips = mesh.shape["seq"] // CORES
    B = 1
    while B * B * 4 <= chips and chips % (B * 2) == 0:
        B *= 2
    A = chips // B
    placed = (
        P(("groups", "seq"), None),
        P(("groups", "seq"), None),
        P(("groups", "seq"), None, None),
        P(("groups", "seq")),
        P("groups", "seq", None),
        P(),
    )
    return jax.shard_map(
        functools.partial(body, A, B),
        mesh=mesh,
        in_specs=placed,
        out_specs=(P(("groups", "seq"), None), P(("groups", "seq"))),
        check_vma=False,
    )
```
